32 devices in a mesh: row: 4 (over y, x), col: 8 (over z, core).
Axes of the slice: x: 2, y: 2, z: 4, core: 2. Of those that a mesh axis runs over, the one named last changes fastest.
Arguments:
- factor_diag: float32 [2, 512, 512], replicated, as said below
- factor_mid: float32 [512, 512], replicated, may hold values from -0.25 to 0.25
- factor_low: float32 [2, 16384, 512], P(None, ('row', 'col')), may hold values from -0.046875 to 0.046875
- adjoint_diag: float32 [2, 512, 512], replicated, may hold values from -6 to 6
- adjoint_mid: float32 [512, 512], replicated, may hold values from -6 to 6
- adjoint_low: float32 [2, 16384, 512], P(None, ('row', 'col')), may hold values from -6 to 6
- trailing_adjoint: float32 [16384, 4, 4096], P('row', None, 'col'), as said below
Outputs:
- grad_diag: float32 [2, 512, 512], replicated
- grad_mid: float32 [512, 512], replicated
- grad_low: float32 [2, 16384, 512], P(None, ('row', 'col'))
The draws below stay inside these ranges and needn't reach their ends.
Inputs may be any that keep to these rules, and one draw needn't show every extreme that they name: `factor_diag`: each of the two [512, 512] blocks is lower triangular with diagonal entries between 1 and 2. `trailing_adjoint`: symmetric when read as an 16384 x 16384 matrix in row-major order.
All inputs are finite; a program needn't handle non-finite values.
Results may differ from the reference program's by a relative error of at most 0.000065.
Values sent between devices are 32-bit elements; how exact they have to be, the bound alone decides.
A program may use at most 192 MiB of HBM per device.

```python
import math
import jax
import jax.numpy as jnp
from jax import lax

B = 512
R = 16384
N_ROW = 4


def draw_factor_diag(key, part):
    first_key, second_key = jax.random.split(jax.random.fold_in(key, 11))
    below = jax.random.normal(first_key, (2, B, B), jnp.float32) * (0.5 / math.sqrt(B))
    main_diag = jax.random.uniform(second_key, (2, B), jnp.float32, 1.0, 2.0)
    identity = jnp.eye(B, dtype=jnp.float32)
    return jnp.tril(below, -1) + main_diag[:, :, None] * identity[None, :, :]


def draw_trailing_adjoint(key, part):
    first_key = jax.random.fold_in(jax.random.fold_in(key, 23), 0)
    base = jax.random.normal(first_key, (R, R), jnp.float32)
    symmetric = (base + base.T) * 0.7071067811865476
    return symmetric.reshape(R, N_ROW, R // N_ROW)


def block_levels(own_key, extent, cuts, low, high):
    gain, own = 1.0, jax.random.fold_in(own_key, 6)
    for dim, parts in cuts:
        steps = jnp.exp(jax.random.uniform(jax.random.fold_in(own, dim), (parts,), jnp.float32, low / len(cuts), high / len(cuts)))
        gain = gain * jnp.repeat(steps, extent[dim] // parts).reshape([-1 if axis == dim else 1 for axis in range(len(extent))])
    return gain


def noise(stream_key, extent, spread, limit, cuts=(), kind=jnp.bfloat16):
    values = spread * jax.random.normal(stream_key, extent, jnp.float32)
    if cuts:
        values = values * block_levels(stream_key, extent, cuts, -0.22, 0.18)
    return jnp.clip(values, -limit, limit).astype(kind)


def setup_inputs(seed: int = 0) -> dict:
    streams_of = jax.random.split(jax.random.key(seed), 8)
    return {
        "factor_diag": draw_factor_diag(jax.random.fold_in(streams_of[7], 71), 0),
        "factor_mid": noise(streams_of[1], (B, B), B ** -0.5, 0.25, (), jnp.float32),
        "factor_low": noise(streams_of[2], (2, R, B), R ** -0.5, 0.046875, ((1, 32),), jnp.float32),
        "adjoint_diag": noise(streams_of[3], (2, B, B), 1.0, 6.0, (), jnp.float32),
        "adjoint_mid": noise(streams_of[4], (B, B), 1.0, 6.0, (), jnp.float32),
        "adjoint_low": noise(streams_of[5], (2, R, B), 1.0, 6.0, ((1, 32),), jnp.float32),
        "trailing_adjoint": draw_trailing_adjoint(jax.random.fold_in(streams_of[7], 71), 0),
    }


def lower_half(matrix):
    return jnp.tril(matrix, -1) + 0.5 * jnp.diag(jnp.diag(matrix))

def product(left_side, right_side):
    return jnp.dot(left_side.astype(jnp.float32), right_side.astype(jnp.float32), precision=lax.Precision.HIGHEST, preferred_element_type=jnp.float32)

def right_solve(factor, row_block):
    return jax.scipy.linalg.solve_triangular(factor, row_block.T, trans=1, lower=True).T

def diag_adjoint(factor, adjoint):
    inner_term = lower_half(product(factor.T, adjoint))
    halfway = jax.scipy.linalg.solve_triangular(factor, inner_term, trans=1, lower=True)
    whole_term = right_solve(factor, halfway)
    return 0.5 * (whole_term + whole_term.T)

def reference(factor_diag, factor_mid, factor_low, adjoint_diag, adjoint_mid, adjoint_low, trailing_adjoint):
    trailing = trailing_adjoint.reshape(R, R)
    second_solved = right_solve(factor_diag[1], adjoint_low[1] - 2.0 * product(trailing, factor_low[1]))
    second_adjoint = adjoint_diag[1] - product(second_solved.T, factor_low[1])
    second_grad = diag_adjoint(factor_diag[1], second_adjoint)
    second_half = 0.5 * second_solved
    top_rows = adjoint_mid - 2.0 * (product(second_grad, factor_mid) + product(second_half.T, factor_low[0]))
    top_solved = right_solve(factor_diag[0], top_rows)
    bottom_rows = adjoint_low[0] - 2.0 * (product(second_half, factor_mid) + product(trailing, factor_low[0]))
    bottom_solved = right_solve(factor_diag[0], bottom_rows)
    first_adjoint = adjoint_diag[0] - product(top_solved.T, factor_mid) - product(bottom_solved.T, factor_low[0])
    first_grad = diag_adjoint(factor_diag[0], first_adjoint)
    return (jnp.stack([first_grad, second_grad]), 0.5 * top_solved, jnp.stack([0.5 * bottom_solved, second_half]))
```

```python
import jax
import jax.numpy as jnp
from jax import lax
from jax.sharding import PartitionSpec as P

LEAF = 128


def product(left_side, right_side, precision=lax.Precision.HIGHEST):
    return jnp.matmul(
        left_side, right_side, precision=precision, preferred_element_type=jnp.float32
    )


def cross(left_side, right_side, precision=lax.Precision.HIGHEST):
    return lax.dot_general(
        left_side,
        right_side,
        (((0,), (0,)), ((), ())),
        precision=precision,
        preferred_element_type=jnp.float32,
    )


def lower_half(matrix):
    rows = lax.broadcasted_iota(jnp.int32, matrix.shape, 0)
    cols = lax.broadcasted_iota(jnp.int32, matrix.shape, 1)
    return jnp.where(rows > cols, matrix, jnp.where(rows == cols, 0.5 * matrix, 0.0))


def lower_inverse(factors):
    count, order, _ = factors.shape
    leaf = min(LEAF, order)
    blocks = jnp.stack(
        [factors[:, i : i + leaf, i : i + leaf] for i in range(0, order, leaf)], axis=1
    ).reshape(-1, leaf, leaf)
    rows = lax.broadcasted_iota(jnp.int32, (leaf, leaf), 0)
    cols = lax.broadcasted_iota(jnp.int32, (leaf, leaf), 1)
    inverse = jnp.where(rows == cols, 1.0 / jnp.where(rows == cols, blocks, 1.0), 0.0)
    size = 1
    while size < leaf:
        corner = (rows // (2 * size) == cols // (2 * size)) & (rows // size > cols // size)
        inner = jnp.where(corner, blocks, 0.0)
        inverse = inverse - product(product(inverse, inner), inverse)
        size *= 2
    pieces = inverse.reshape(count, order // leaf, leaf, leaf)
    while size < order:
        pairs = order // (2 * size)
        first, second = pieces[:, 0::2], pieces[:, 1::2]
        corner = jnp.stack(
            [
                factors[:, (2 * i + 1) * size : (2 * i + 2) * size, 2 * i * size : (2 * i + 1) * size]
                for i in range(pairs)
            ],
            axis=1,
        )
        below = -product(product(second, corner), first)
        pieces = jnp.concatenate(
            [
                jnp.concatenate([first, jnp.zeros_like(first)], axis=3),
                jnp.concatenate([below, second], axis=3),
            ],
            axis=2,
        )
        size *= 2
    return pieces[:, 0]


def swap(value, axis, size, offset):
    return lax.ppermute(value, axis, [(i, i ^ offset) for i in range(size)])


def place(buffer, index, value):
    return lax.dynamic_update_slice_in_dim(buffer, value[None], index, 0)


def pick(buffer, index):
    return lax.dynamic_index_in_dim(buffer, index, 0, keepdims=False)


def gather(value, axis, size, step=1):
    count = size // step
    me = lax.axis_index(axis)
    slot = me // step
    arrived = [swap(value, axis, size, j * step) for j in range(1, count)]
    held = jnp.zeros((count,) + value.shape, value.dtype)
    held = place(held, slot, value)
    for j in range(1, count):
        held = place(held, slot ^ j, arrived[j - 1])
    return held


def scatter(parts, axis, size, step=1):
    count = size // step
    slot = lax.axis_index(axis) // step
    total = pick(parts, slot)
    for j in range(1, count):
        total = total + swap(pick(parts, slot ^ j), axis, size, j * step)
    return total


def total_over(value, n_row, n_col):
    core = lax.axis_index("col") % 2
    halves = value.reshape((2, -1) + value.shape[1:])
    mine = pick(halves, core) + swap(pick(halves, 1 - core), "col", n_col, 1)
    shape = mine.shape
    part = scatter(mine.reshape((n_row, -1) + shape[1:]), "row", n_row)
    part = scatter(part.reshape((n_col // 2, -1) + shape[1:]), "col", n_col, 2)
    part = gather(part, "col", n_col, 2).reshape((-1,) + shape[1:])
    part = gather(part, "row", n_row).reshape(shape)
    other = swap(part, "col", n_col, 1)
    lower = jnp.where(core == 0, part, other)
    upper = jnp.where(core == 0, other, part)
    return jnp.concatenate([lower, upper], axis=0)


def diag_adjoint(factor, inverse, adjoint):
    inner_term = lower_half(cross(factor, adjoint))
    whole_term = product(cross(inverse, inner_term), inverse)
    return 0.5 * (whole_term + whole_term.T)


def solution(mesh):
    n_row, n_col = mesh.shape["row"], mesh.shape["col"]

    def shards(
        factor_diag, factor_mid, factor_low, adjoint_diag, adjoint_mid, adjoint_low, trailing_adjoint
    ):
        block_rows, row_groups, group_cols = trailing_adjoint.shape
        width = factor_mid.shape[0]
        high = lax.Precision.HIGH
        local_block = trailing_adjoint.reshape(block_rows, row_groups * group_cols)
        columns = gather(factor_low[1], "row", n_row).reshape(-1, width)
        chips = gather(factor_low[0], "col", n_col, 2)
        inverses = lower_inverse(factor_diag)
        local_block, columns, chips, inverses = lax.optimization_barrier(
            (local_block, columns, chips, inverses)
        )
        second_image = lax.psum_scatter(
            product(local_block, columns, high), "col", scatter_dimension=0, tiled=True
        )
        core = lax.axis_index("col") % 2
        other = swap(chips, "col", n_col, 1)
        rows = jnp.stack(
            [jnp.where(core == 0, chips, other), jnp.where(core == 0, other, chips)], axis=1
        ).reshape(-1, width)
        partial = cross(local_block, rows, high).reshape(row_groups, group_cols, width)
        first_image = scatter(partial, "row", n_row)

        second_rows = adjoint_low[1] - 2.0 * second_image
        first_rows = adjoint_low[0] - 2.0 * first_image
        terms = jnp.concatenate(
            [
                cross(second_rows, factor_low[1]),
                cross(second_rows, factor_low[0]),
                cross(first_rows, factor_low[0]),
            ],
            axis=0,
        )
        totals = total_over(terms, n_row, n_col)

        second_solved = product(second_rows, inverses[1])
        second_half = 0.5 * second_solved
        bottom_solved = product(first_rows - product(second_solved, factor_mid), inverses[0])

        second_total = cross(inverses[1], totals[:width])
        upper_total = 0.5 * cross(inverses[1], totals[width : 2 * width])
        lower_total = cross(inverses[0], totals[2 * width :] - 2.0 * cross(factor_mid, upper_total))
        second_grad = diag_adjoint(factor_diag[1], inverses[1], adjoint_diag[1] - second_total)
        top_rows = adjoint_mid - 2.0 * (product(second_grad, factor_mid) + upper_total)
        top_solved = product(top_rows, inverses[0])
        first_adjoint = adjoint_diag[0] - cross(top_solved, factor_mid) - lower_total
        first_grad = diag_adjoint(factor_diag[0], inverses[0], first_adjoint)
        return (
            jnp.stack([first_grad, second_grad]),
            0.5 * top_solved,
            jnp.stack([0.5 * bottom_solved, second_half]),
        )

    return jax.shard_map(
        shards,
        mesh=mesh,
        in_specs=(
            P(),
            P(),
            P(None, ("row", "col"), None),
            P(),
            P(),
            P(None, ("row", "col"), None),
            P("row", None, "col"),
        ),
        out_specs=(P(), P(), P(None, ("row", "col"), None)),
        check_vma=False,
    )
```
